32 devices in a mesh: band: 8 (over z, y), slab: 4 (over x, core).
Axes of the slice: x: 2, y: 2, z: 4, core: 2. Of those that a mesh axis runs over, the one named last changes fastest.
Arguments:
- orbitals: bfloat16 [32, 160, 160, 160], P('band', 'slab'), may hold values from -4 to 4
- owner: int32 [2], replicated, may hold values from 0 to 7, as said below
- index: int32 [2], replicated, may hold values from 0 to 3, as said below
Outputs:
- exchange: bfloat16 [32, 160, 160, 160], P('band', 'slab')
The draws below stay inside these ranges and needn't reach their ends.
Inputs may be any that keep to these rules, and one draw needn't show every extreme that they name: `owner`: the two partners lie in different band groups, one of them in the last group. `index`: the two positions differ, one of them is the last position of a block.
All inputs are finite; a program needn't handle non-finite values.
Results may differ from the reference program's by a relative error of at most 0.0022.
Values may be sent and summed in bfloat16 or wider, within the bound.
No kernel may reach another device: no remote copies, remote signals or barrier semaphores. Data moves between devices by JAX's collectives and lax.ppermute only.
A program may use at most 256 MiB of HBM per device.

```python
import math
import jax
import jax.numpy as jnp
from jax import lax

NX = 160
NY = 160
NZ = 160
BLK = 4
NORB = 32
N_BAND = 8


def draw_orbitals(key, part):
    shape = (NORB, NZ, NX, NY)
    return jax.random.truncated_normal(key, -4.0, 4.0, shape, jnp.float32).astype(jnp.bfloat16)


def pair_with_top(key, count):
    other = jax.random.randint(jax.random.fold_in(key, 1), (), 0, count - 1, dtype=jnp.int32)
    flip = jax.random.randint(jax.random.fold_in(key, 2), (), 0, 2, dtype=jnp.int32)
    top = jnp.int32(count - 1)
    first = jnp.where(flip == 1, other, top)
    second = jnp.where(flip == 1, top, other)
    return jnp.stack([first, second]).astype(jnp.int32)


def draw_owner(key, part):
    return pair_with_top(jax.random.fold_in(key, 101), N_BAND)


def draw_index(key, part):
    return pair_with_top(jax.random.fold_in(key, 202), BLK)


def setup_inputs(seed: int = 0) -> dict:
    key_of = jax.random.split(jax.random.key(seed), 4)
    return {
        "orbitals": draw_orbitals(jax.random.fold_in(key_of[3], 71), 0),
        "owner": draw_owner(jax.random.fold_in(key_of[3], 71), 0),
        "index": draw_index(jax.random.fold_in(key_of[3], 71), 0),
    }


spacing = 0.293125


def hartley(grid):
    for axis in range(3):
        spectrum = jnp.fft.fft(grid, axis=axis)
        grid = (spectrum.real - spectrum.imag).astype(grid.dtype)
    return grid


def squared_wave(count):
    steps = jnp.arange(count, dtype=jnp.int32)
    folded = jnp.where(steps <= count // 2, steps, steps - count).astype(jnp.float32)
    wave = 2.0 * math.pi * folded / (count * spacing)
    return wave * wave


def coulomb():
    g_sq = squared_wave(NZ)[:, None, None] + squared_wave(NX)[None, :, None] + squared_wave(NY)[None, None, :]
    safe = jnp.where(g_sq > 0, g_sq, jnp.float32(1.0))
    return jnp.where(g_sq > 0, 4.0 * math.pi / safe, jnp.float32(0.0)) / (NX * NY * NZ)


def reference(orbitals, owner, index):
    kernel = coulomb()
    total = jnp.zeros((NORB, NZ, NX, NY), jnp.float32)
    for which in range(2):
        row = (owner[which] * BLK + index[which]).astype(jnp.int32)
        partner = lax.dynamic_index_in_dim(orbitals, row, 0, keepdims=False).astype(jnp.float32)

        def one_band(band):
            density = band.astype(jnp.float32) * partner
            potential = hartley(kernel * hartley(density))
            return partner * potential

        total = total + lax.map(one_band, orbitals)
    return (-0.25 * total).astype(jnp.bfloat16)
```

```python
import math

import jax
import jax.numpy as jnp
import ml_dtypes
import numpy as np
from jax import lax
from jax.experimental import pallas as pl
from jax.experimental.pallas import tpu as pltpu
from jax.sharding import PartitionSpec as P

spacing = 0.293125
exact = lax.Precision.HIGHEST
LANES = 128
TAIL = 32
FOLD = LANES // TAIL
VMEM = 56 * 2**20
bf16, f32 = jnp.bfloat16, jnp.float32


def cas_np(count):
    steps = np.arange(count)
    angle = 2.0 * np.pi / count * (steps[:, None] * steps[None, :] % count)
    return np.cos(angle) + np.sin(angle)


def split_np(table):
    high = table.astype(ml_dtypes.bfloat16)
    low = (table - high.astype(np.float64)).astype(ml_dtypes.bfloat16)
    return high, low


def wave_np(count):
    steps = np.arange(count)
    folded = np.where(steps <= count // 2, steps, steps - count)
    return (2.0 * np.pi * folded / (count * spacing)) ** 2


def right_table(count):
    high, low = split_np(cas_np(count))
    wide = [np.concatenate([t[:, :LANES]] + [t[:, LANES:]] * FOLD, axis=1) for t in (high, low)]
    high, low = wide
    zero = np.zeros_like(high[LANES:])
    return np.concatenate(
        [high[:LANES], high[:LANES], low[:LANES], high[LANES:], high[LANES:], low[LANES:], zero]
    )


def packed_wave(width, across):
    sq = wave_np(width)[:, None] + wave_np(across)[None, :]
    tails = sq[:, LANES:].reshape(FOLD, width // FOLD, TAIL).transpose(1, 0, 2)
    return np.concatenate([sq[:, :LANES], tails.reshape(width // FOLD, LANES)]).astype(np.float32)


def halves(value):
    high = value.astype(bf16)
    low = (value - high.astype(f32)).astype(bf16)
    return high, low


def lane_group():
    return lax.broadcasted_iota(jnp.int32, (1, LANES), 1) // TAIL


def spread_tails(packed):
    group = lane_group()
    turned = [packed] + [pltpu.roll(packed, TAIL * k, axis=1) for k in range(1, FOLD)]
    out = []
    for q in range(FOLD):
        rows = turned[(0 - q) % FOLD]
        for g in range(1, FOLD):
            rows = jnp.where(group == g, turned[(g - q) % FOLD], rows)
        out.append(rows)
    return jnp.concatenate(out, axis=0)


def gather_tails(tails):
    group = lane_group()
    rows = tails.shape[0] // FOLD
    packed = tails[:rows]
    for q in range(1, FOLD):
        packed = jnp.where(group == q, tails[q * rows : (q + 1) * rows], packed)
    return packed


def right_operand(main, tails):
    main_high, main_low = halves(main)
    tail_high, tail_low = halves(tails)
    mixed = jnp.where(lane_group() == 1, tail_low.astype(f32), tail_high.astype(f32)).astype(bf16)
    return jnp.concatenate([main_high, main_low, main_high, mixed], axis=1)


def left_product(table, value):
    high, low = halves(value)
    stacked = jnp.concatenate([high, low, high], axis=0)
    return jnp.dot(table, stacked, preferred_element_type=f32)


def pack_kernel(count, pick_ref, x_ref, *out_refs):
    planes, width = x_ref.shape[1], x_ref.shape[2]
    quarter = width // FOLD
    lane = lax.broadcasted_iota(jnp.int32, (TAIL, LANES), 1)
    row = lax.broadcasted_iota(jnp.int32, (TAIL, LANES), 0)
    for n in range(count):
        which = pick_ref[n]
        for p in range(planes):
            plane = x_ref[which, p]
            out_refs[n][p, :width, :] = plane[:, :LANES]
            tails = plane[:, LANES:]
            packed = None
            for q in range(FOLD):
                place = (lane == row + TAIL * q).astype(f32).astype(bf16)
                moved = jnp.dot(tails, place, preferred_element_type=f32)
                moved = moved[q * quarter : (q + 1) * quarter]
                packed = moved if packed is None else packed + moved
            out_refs[n][p, width:, :] = packed.astype(bf16)


def pack(orbitals, picks, planes=4):
    block, depth, width, across = orbitals.shape
    rows = width + width // FOLD
    count = picks.shape[0]

    def kernel(*refs):
        pack_kernel(count, *refs)

    return pl.pallas_call(
        kernel,
        grid_spec=pltpu.PrefetchScalarGridSpec(
            num_scalar_prefetch=1,
            grid=(depth // planes,),
            in_specs=[pl.BlockSpec((block, planes, width, across), lambda i, p: (0, i, 0, 0))],
            out_specs=[pl.BlockSpec((planes, rows, LANES), lambda i, p: (i, 0, 0))] * count,
        ),
        out_shape=[jax.ShapeDtypeStruct((depth, rows, LANES), bf16)] * count,
        compiler_params=pltpu.CompilerParams(vmem_limit_bytes=VMEM),
    )(picks, orbitals)


def forward_kernel(width, first, chunk_ref, *refs):
    o_refs, (u_ref, v_ref, right_ref, left_ref) = refs[:4], refs[4:8]
    s_ref, p_ref = refs[-2:]
    right, left = right_ref[...], left_ref[...]
    lhs = []
    for d in range(4):
        orbital = o_refs[d][0].astype(f32)
        for j in range(2):
            partner = (u_ref, v_ref)[d % 2][d // 2, j, 0]
            p_ref[j, d, 0] = partner
            density = orbital * partner.astype(f32)
            lhs.append(right_operand(density[:width], spread_tails(density[width:])))
    along_y = jnp.dot(jnp.concatenate(lhs, axis=0), right, preferred_element_type=f32)
    for n in range(8):
        value = left_product(left, along_y[n * width : (n + 1) * width])
        s_ref[n % 2, n // 2, 0, :width, :] = value[:, :LANES]
        s_ref[n % 2, n // 2, 0, width:, :] = gather_tails(value[:, LANES:])


def forward(chunk, orbitals, unit, other, right, left, held, width):
    depth, rows, _ = orbitals[0].shape
    planes = unit.shape[2]
    plane = lambda i, c: (c[0] * planes + i, 0, 0)
    whole = lambda i, c: (0, 0)
    part = lambda i, c: (0, 0, i, 0, 0)
    out = lambda i, c: (0, 0, c[0] * planes + i, 0, 0)
    in_specs = (
        [pl.BlockSpec((1, rows, LANES), plane)] * 4
        + [pl.BlockSpec((2, 2, 1, rows, LANES), part)] * 2
        + [pl.BlockSpec(right.shape, whole), pl.BlockSpec(left.shape, whole)]
    )
    args = [*orbitals, unit, other, right, left]
    alias = {}
    if held is not None:
        in_specs += [pl.BlockSpec(memory_space=pl.ANY)] * 2
        alias = {1 + len(args): 0, 2 + len(args): 1}
        args += list(held)

    def kernel(*refs):
        forward_kernel(width, held is None, *refs)

    return pl.pallas_call(
        kernel,
        grid_spec=pltpu.PrefetchScalarGridSpec(
            num_scalar_prefetch=1,
            grid=(planes,),
            in_specs=in_specs,
            out_specs=[pl.BlockSpec((2, 4, 1, rows, LANES), out)] * 2,
        ),
        out_shape=[
            jax.ShapeDtypeStruct((2, 4, depth, rows, LANES), f32),
            jax.ShapeDtypeStruct((2, 4, depth, rows, LANES), bf16),
        ],
        input_output_aliases=alias,
        compiler_params=pltpu.CompilerParams(vmem_limit_bytes=VMEM),
    )(jnp.reshape(chunk, (1,)).astype(jnp.int32), *args)


def middle_kernel(scale, x_ref, wave_ref, depth_ref, ahead_ref, back_ref, o_ref):
    depth = x_ref.shape[1] * x_ref.shape[2]
    group = x_ref.shape[3]
    flat = x_ref.reshape(2 * depth * group, LANES)
    result = o_ref.reshape(2 * depth * group, LANES)
    along_z = depth_ref[...]
    kernel = []
    for r in range(group):
        g_sq = along_z + wave_ref[r : r + 1, :]
        safe = jnp.where(g_sq > 0, g_sq, 1.0)
        kernel.append(jnp.where(g_sq > 0, scale / safe, 0.0))
    kernel = jnp.concatenate(kernel, axis=1)
    for j in range(2):
        first = j * depth * group
        parts = [flat[pl.ds(first + r, depth, stride=group), :] for r in range(group)]
        value = left_product(ahead_ref[...], jnp.concatenate(parts, axis=1)) * kernel
        value = left_product(back_ref[...], value)
        for r in range(group):
            result[pl.ds(first + r, depth, stride=group), :] = value[:, r * LANES : (r + 1) * LANES]


def middle(spectrum, wave, along_z, ahead, back, scale, group=8):
    _, slabs, depth, rows, _ = spectrum.shape
    block = pl.BlockSpec((2, slabs, depth, group, LANES), lambda i: (0, 0, 0, i, 0))
    whole = lambda i: (0, 0)

    def kernel(*refs):
        middle_kernel(scale, *refs)

    return pl.pallas_call(
        kernel,
        grid=(rows // group,),
        in_specs=[
            block,
            pl.BlockSpec((group, LANES), lambda i: (i, 0)),
            pl.BlockSpec(along_z.shape, whole),
            pl.BlockSpec(ahead.shape, whole),
            pl.BlockSpec(back.shape, whole),
        ],
        out_specs=block,
        out_shape=jax.ShapeDtypeStruct(spectrum.shape, f32),
        input_output_aliases={0: 0},
        compiler_params=pltpu.CompilerParams(vmem_limit_bytes=VMEM),
    )(spectrum, wave, along_z, ahead, back)


def backward_kernel(width, v_ref, p_ref, right_ref, left_ref, o_ref):
    planes = v_ref.shape[2]
    right, left = right_ref[...], left_ref[...]
    lhs = []
    for p in range(planes):
        for j in range(2):
            packed = v_ref[j, 0, p]
            value = jnp.concatenate([packed[:width], spread_tails(packed[width:])], axis=1)
            value = left_product(left, value)
            lhs.append(right_operand(value[:, :LANES], value[:, LANES:]))
    values = jnp.dot(jnp.concatenate(lhs, axis=0), right, preferred_element_type=f32)
    for p in range(planes):
        main, tail = 0.0, 0.0
        for j in range(2):
            n = 2 * p + j
            value = values[n * width : (n + 1) * width]
            partner = p_ref[j, 0, p].astype(f32)
            main = main + value[:, :LANES] * partner[:width]
            tail = tail + gather_tails(value[:, LANES:]) * partner[width:]
        o_ref[p, :width, :] = main.astype(bf16)
        o_ref[p, width:, :] = tail.astype(bf16)


def backward(potential, partners, right, left, slab, width, planes=4):
    _, _, depth, rows, _ = potential.shape
    block = pl.BlockSpec((2, 1, planes, rows, LANES), lambda i: (0, slab, i, 0, 0))
    whole = lambda i: (0, 0)

    def kernel(*refs):
        backward_kernel(width, *refs)

    return pl.pallas_call(
        kernel,
        grid=(depth // planes,),
        in_specs=[block, block, pl.BlockSpec(right.shape, whole), pl.BlockSpec(left.shape, whole)],
        out_specs=pl.BlockSpec((planes, rows, LANES), lambda i: (i, 0, 0)),
        out_shape=jax.ShapeDtypeStruct((depth, rows, LANES), bf16),
        compiler_params=pltpu.CompilerParams(vmem_limit_bytes=VMEM),
    )(potential, partners, right, left)


def unpack_kernel(pick_ref, x_ref, *refs):
    o_ref = refs[-1]
    planes, width = o_ref.shape[1], o_ref.shape[2]
    for p in range(planes):
        o_ref[0, p, :, :LANES] = x_ref[p, :width, :]
        packed = x_ref[p, width:, :].astype(f32)
        parts = [packed] + [pltpu.roll(packed, LANES - TAIL * q, axis=1) for q in range(1, FOLD)]
        tails = jnp.concatenate(parts, axis=0).astype(bf16)
        o_ref[0, p, :, LANES:] = tails[:, :TAIL]


def unpack(piece, which, held, shape, planes=8):
    block, depth, width, across = shape
    rows = piece.shape[1]
    in_specs = [pl.BlockSpec((planes, rows, LANES), lambda i, w: (i, 0, 0))]
    args, alias = [piece], {}
    if held is not None:
        in_specs.append(pl.BlockSpec(memory_space=pl.ANY))
        args.append(held)
        alias = {2: 0}
    return pl.pallas_call(
        unpack_kernel,
        grid_spec=pltpu.PrefetchScalarGridSpec(
            num_scalar_prefetch=1,
            grid=(depth // planes,),
            in_specs=in_specs,
            out_specs=pl.BlockSpec((1, planes, width, across), lambda i, w: (w[0], i, 0, 0)),
        ),
        out_shape=jax.ShapeDtypeStruct(shape, bf16),
        input_output_aliases=alias,
        compiler_params=pltpu.CompilerParams(vmem_limit_bytes=VMEM),
    )(jnp.reshape(which, (1,)).astype(jnp.int32), *args)


def swap(value, bit):
    count = lax.axis_size("slab")
    return lax.ppermute(value, "slab", [(i, i ^ bit) for i in range(count)])


def ring_order(count):
    return list(range(0, count, 2)) + list(range(count - 1, 0, -2))


def turn(value, step):
    order = ring_order(lax.axis_size("band"))
    count = len(order)
    pairs = [(order[i], order[(i + step) % count]) for i in range(count)]
    return lax.ppermute(value, "band", pairs)


def scatter(piece, mine, place, count, step):
    planes = piece.shape[0] // count

    def own(offset):
        chunk = (place + offset) % count
        return lax.dynamic_slice_in_dim(piece, chunk * planes, planes, 0)

    moving = own(-step)
    for hop in range(1, count):
        moving = turn(moving, step)
        moving = jnp.where(mine, own(-step * (hop + 1)), moving)
    return moving


def whole_orbital(orbitals, owner, index):
    block, depth_local, width, across = orbitals.shape
    slabs, bands = lax.axis_size("slab"), lax.axis_size("band")
    depth = depth_local * slabs
    me, band = lax.axis_index("slab"), lax.axis_index("band")
    order = ring_order(bands)
    place = jnp.asarray(np.argsort(order).astype(np.int32))[band]

    right = jnp.asarray(right_table(across))
    high, low = split_np(cas_np(width))
    left = jnp.asarray(np.concatenate([high, high, low], axis=1))
    high, low = split_np(cas_np(depth))
    wave = jnp.asarray(packed_wave(width, across))
    along_z = jnp.asarray(np.tile(wave_np(depth)[:, None], (1, LANES)).astype(np.float32))
    turned = me ^ jnp.arange(slabs, dtype=jnp.int32)

    def in_columns(table):
        parts = jnp.asarray(table).reshape(depth, slabs, depth_local)
        return jnp.take(parts, turned, axis=1).reshape(depth, depth)

    def in_rows(table):
        parts = jnp.asarray(table).reshape(slabs, depth_local, depth)
        return jnp.take(parts, turned, axis=0).reshape(depth, depth)

    ahead = jnp.concatenate([in_columns(high), in_columns(high), in_columns(low)], axis=1)
    back = jnp.concatenate([in_rows(high), in_rows(high), in_rows(low)], axis=1)

    candidates = pack(orbitals, index)
    pieces = pack(orbitals, turned)
    mine = [owner[j] == band for j in range(2)]
    chunks = [scatter(candidates[j], mine[j], place, bands, (1, -1)[j]) for j in range(2)]
    orbital = [pieces[0]] + [swap(pieces[d], d) for d in range(1, slabs)]
    chunk = jnp.stack(chunks)
    unit = jnp.stack([chunk, swap(chunk, 2)])

    held = None

    def work(offset, unit):
        nonlocal held
        where = (place + offset) % bands
        held = forward(where, orbital, unit, swap(unit, 1), right, left, held, width)

    up, down = unit, unit
    arrived = [(0, unit)]
    for hop in range(1, bands // 2):
        up, down = turn(up, 1), turn(down, -1)
        arrived += [(-hop, up), (hop, down)]
    last = jnp.stack([turn(up[0], 1), turn(down[1], -1)])
    arrived.append((bands // 2, last))
    for offset, value in arrived:
        work(offset, value)

    spectrum, partners = held
    scale = -0.25 * 4.0 * math.pi / (depth * width * across)
    potential = middle(spectrum, wave, along_z, ahead, back, scale)

    out = None
    done = {}
    for d in (2, 3, 1, 0):
        total = backward(potential, partners, right, left, d, width)
        done[d] = swap(total, d) if d else total
    for d in (0, 1, 2, 3):
        out = unpack(done[d], turned[d], out, orbitals.shape)
    return out


def spread(block, axis, source):
    block = jnp.where(lax.axis_index(axis) == source, block, jnp.zeros_like(block))
    return lax.psum(block, axis)


def cas_table(count):
    steps = jnp.arange(count, dtype=jnp.int32)
    product = steps[:, None] * steps[None, :] % count
    angle = 2.0 * math.pi / count * product.astype(jnp.float32)
    return jnp.cos(angle) + jnp.sin(angle)


def squared_wave(steps, count):
    folded = jnp.where(steps <= count // 2, steps, steps - count).astype(jnp.float32)
    wave = 2.0 * math.pi * folded / (count * spacing)
    return wave * wave


def coulomb_slice(depth, first, width, across):
    along_z = squared_wave(jnp.arange(depth, dtype=jnp.int32), depth)
    along_x = squared_wave(
        first + jnp.arange(width, dtype=jnp.int32), width * lax.axis_size("slab")
    )
    along_y = squared_wave(jnp.arange(across, dtype=jnp.int32), across)
    g_sq = along_z[:, None, None] + along_x[None, :, None] + along_y[None, None, :]
    safe = jnp.where(g_sq > 0, g_sq, jnp.float32(1.0))
    whole = depth * width * lax.axis_size("slab") * across
    return jnp.where(g_sq > 0, 4.0 * math.pi / safe, jnp.float32(0.0)) / whole


def along_x(grid, table):
    return jnp.einsum(
        "pzxy,xk->pzky", grid, table, precision=exact, preferred_element_type=jnp.float32
    )


def along_y(grid, table):
    return jnp.einsum(
        "pzxy,yk->pzxk", grid, table, precision=exact, preferred_element_type=jnp.float32
    )


def along_z(grid, table):
    return jnp.einsum(
        "pzxy,zk->pkxy", grid, table, precision=exact, preferred_element_type=jnp.float32
    )


def fetch(orbitals, owner, index, which):
    local = lax.dynamic_index_in_dim(orbitals, index[which], 0, keepdims=False)
    return spread(local, "band", owner[which])


def solve(density, tables, kernel):
    table_x, table_y, table_z = tables
    spectrum = along_x(density, table_x)
    spectrum = along_y(spectrum, table_y)
    scaled = (
        along_z(lax.all_to_all(spectrum, "slab", split_axis=2, concat_axis=1, tiled=True), table_z)
        * kernel[None]
    )
    back = along_z(scaled, table_z)
    potential = lax.all_to_all(back, "slab", split_axis=1, concat_axis=2, tiled=True)
    potential = along_y(potential, table_y)
    return along_x(potential, table_x)


def split_orbital(orbitals, owner, index):
    block, depth_local, width, across = orbitals.shape
    slabs = lax.axis_size("slab")
    depth = depth_local * slabs
    width_local = width // slabs
    tables = (cas_table(width), cas_table(across), cas_table(depth))
    first = lax.axis_index("slab") * width_local
    kernel = coulomb_slice(depth, first, width_local, across)
    bands = orbitals.astype(jnp.float32)
    total = jnp.zeros(orbitals.shape, jnp.float32)
    for which in range(2):
        partner = fetch(orbitals, owner, index, which).astype(jnp.float32)
        potential = solve(bands * partner[None], tables, kernel)
        total = total + partner[None] * potential
    return (-0.25 * total).astype(jnp.bfloat16)


def per_device(orbitals, owner, index):
    block, depth_local, width, across = orbitals.shape
    slabs, bands = lax.axis_size("slab"), lax.axis_size("band")
    fits = (
        block == slabs == 4
        and bands % 2 == 0
        and depth_local % bands == 0
        and depth_local % 8 == 0
        and across == LANES + TAIL
        and width % (8 * FOLD) == 0
    )
    return (whole_orbital if fits else split_orbital)(orbitals, owner, index)


def solution(mesh):
    placed = (P("band", "slab", None, None), P(), P())
    return jax.shard_map(
        per_device,
        mesh=mesh,
        in_specs=placed,
        out_specs=P("band", "slab", None, None),
        check_vma=False,
    )
```

```python
import math

import jax
import jax.numpy as jnp
import ml_dtypes
import numpy as np
from jax import lax
from jax.experimental import pallas as pl
from jax.experimental.pallas import tpu as pltpu
from jax.sharding import PartitionSpec as P

spacing = 0.293125
exact = lax.Precision.HIGHEST
LANES = 128
TAIL = 32
FOLD = LANES // TAIL
VMEM = 56 * 2**20
bf16, f32 = jnp.bfloat16, jnp.float32


def cas_np(count):
    steps = np.arange(count)
    angle = 2.0 * np.pi / count * (steps[:, None] * steps[None, :] % count)
    return np.cos(angle) + np.sin(angle)


def split_np(table):
    high = table.astype(ml_dtypes.bfloat16)
    low = (table - high.astype(np.float64)).astype(ml_dtypes.bfloat16)
    return high, low


def wave_np(count):
    steps = np.arange(count)
    folded = np.where(steps <= count // 2, steps, steps - count)
    return (2.0 * np.pi * folded / (count * spacing)) ** 2


def right_table(count):
    high, low = split_np(cas_np(count))
    wide = [np.concatenate([t[:, :LANES]] + [t[:, LANES:]] * FOLD, axis=1) for t in (high, low)]
    high, low = wide
    zero = np.zeros_like(high[LANES:])
    return np.concatenate(
        [high[:LANES], high[:LANES], low[:LANES], high[LANES:], high[LANES:], low[LANES:], zero]
    )


def packed_wave(width, across):
    sq = wave_np(width)[:, None] + wave_np(across)[None, :]
    tails = sq[:, LANES:].reshape(FOLD, width // FOLD, TAIL).transpose(1, 0, 2)
    return np.concatenate([sq[:, :LANES], tails.reshape(width // FOLD, LANES)]).astype(np.float32)


def halves(value):
    high = value.astype(bf16)
    low = (value - high.astype(f32)).astype(bf16)
    return high, low


def lane_group():
    return lax.broadcasted_iota(jnp.int32, (1, LANES), 1) // TAIL


def spread_tails(packed):
    group = lane_group()
    turned = [packed] + [pltpu.roll(packed, TAIL * k, axis=1) for k in range(1, FOLD)]
    out = []
    for q in range(FOLD):
        rows = turned[(0 - q) % FOLD]
        for g in range(1, FOLD):
            rows = jnp.where(group == g, turned[(g - q) % FOLD], rows)
        out.append(rows)
    return jnp.concatenate(out, axis=0)


def gather_tails(tails):
    group = lane_group()
    rows = tails.shape[0] // FOLD
    packed = tails[:rows]
    for q in range(1, FOLD):
        packed = jnp.where(group == q, tails[q * rows : (q + 1) * rows], packed)
    return packed


def right_operand(main, tails):
    high, low = halves(main)
    coarse = tails.astype(bf16).astype(f32)
    mixed = (tails - jnp.where(lane_group() == 1, coarse, 0.0)).astype(bf16)
    return jnp.concatenate([high, low, high, mixed], axis=1)


def left_product(table, value):
    high, low = halves(value)
    stacked = jnp.concatenate([high, low, high], axis=0)
    return jnp.dot(table, stacked, preferred_element_type=f32)


def pack_kernel(pick_ref, *refs):
    count = len(refs) // 2
    planes, width = refs[0].shape[1], refs[0].shape[2]
    lane = lax.broadcasted_iota(jnp.int32, (TAIL, LANES), 1)
    row = lax.broadcasted_iota(jnp.int32, (TAIL, LANES), 0)
    place = (lane % TAIL == row).astype(f32).astype(bf16)
    for x_ref, o_ref in zip(refs[:count], refs[count:]):
        tails = x_ref[0, :, :, LANES:].reshape(planes * width, TAIL)
        tails = jnp.dot(tails, place, preferred_element_type=f32)
        for p in range(planes):
            o_ref[p, :width, :] = x_ref[0, p, :, :LANES]
            o_ref[p, width:, :] = gather_tails(tails[p * width : (p + 1) * width]).astype(bf16)


def pack(orbitals, picks, planes=20):
    block, depth, width, across = orbitals.shape
    rows = width + width // FOLD
    count = picks.shape[0]

    def picked(n):
        return pl.BlockSpec((1, planes, width, across), lambda i, p: (p[n], i, 0, 0))

    return pl.pallas_call(
        pack_kernel,
        grid_spec=pltpu.PrefetchScalarGridSpec(
            num_scalar_prefetch=1,
            grid=(depth // planes,),
            in_specs=[picked(n) for n in range(count)],
            out_specs=[pl.BlockSpec((planes, rows, LANES), lambda i, p: (i, 0, 0))] * count,
        ),
        out_shape=[jax.ShapeDtypeStruct((depth, rows, LANES), bf16)] * count,
        compiler_params=pltpu.CompilerParams(vmem_limit_bytes=VMEM),
    )(picks, *[orbitals] * count)


def forward_kernel(width, count, places_ref, *refs):
    o_refs, p_refs, (right_ref, left_ref, s_ref) = refs[:count], refs[count : 2 * count], refs[-3:]
    right, left = right_ref[...], left_ref[...]
    lhs = []
    for o_ref, p_ref in zip(o_refs, p_refs):
        density = o_ref[0].astype(f32) * p_ref[0, 0].astype(f32)
        lhs.append(right_operand(density[:width], spread_tails(density[width:])))
    for n in range(count):
        along_y = jnp.dot(lhs[n], right, preferred_element_type=f32)
        value = left_product(left, along_y)
        s_ref[n, 0, :width, :] = value[:, :LANES]
        s_ref[n, 0, width:, :] = gather_tails(value[:, LANES:])


def costs(pairs, width, moved):
    flops = int(pairs * width * 2 * 2 * 3 * 256 * 160 * 1.5)
    return pl.CostEstimate(flops=flops, bytes_accessed=int(moved), transcendentals=0)


def forward(places, orbital, partner, right, left, width):
    rows = orbital.shape[1]
    count, planes = len(partner), partner[0][0].shape[1]
    whole = lambda i, c: (0, 0)

    def at(n):
        return pl.BlockSpec((1, rows, LANES), lambda i, c: (c[n] * planes + i, 0, 0))

    def of(part):
        return pl.BlockSpec((1, 1, rows, LANES), lambda i, c: (part, i, 0, 0))

    def kernel(*refs):
        forward_kernel(width, count, *refs)

    shape = (count, planes, rows, LANES)
    return pl.pallas_call(
        kernel,
        grid_spec=pltpu.PrefetchScalarGridSpec(
            num_scalar_prefetch=1,
            grid=(planes,),
            in_specs=[at(n) for n in range(count)]
            + [of(part) for _, part in partner]
            + [pl.BlockSpec(right.shape, whole), pl.BlockSpec(left.shape, whole)],
            out_specs=pl.BlockSpec((count, 1, rows, LANES), lambda i, c: (0, i, 0, 0)),
        ),
        out_shape=jax.ShapeDtypeStruct(shape, f32),
        cost_estimate=costs(count * planes, width, 8 * math.prod(shape)),
        compiler_params=pltpu.CompilerParams(vmem_limit_bytes=VMEM),
    )(places, *[orbital] * count, *[array for array, _ in partner], right, left)


def middle_kernel(scale, slabs, *refs):
    x_refs, (wave_ref, depth_ref, ahead_ref, back_ref) = refs[:slabs], refs[slabs : slabs + 4]
    o_refs = refs[slabs + 4 :]
    chunks, planes, group, _ = x_refs[0].shape
    local = chunks * planes
    along_z = depth_ref[...]
    sources = [ref.reshape(local * group, LANES) for ref in x_refs]
    results = [ref.reshape(local * group, LANES) for ref in o_refs]
    for first in range(0, group, 8):
        kernel, parts = [], []
        for r in range(first, first + 8):
            g_sq = along_z + wave_ref[r : r + 1, :]
            safe = jnp.where(g_sq > 0, g_sq, 1.0)
            kernel.append(jnp.where(g_sq > 0, scale / safe, 0.0))
            rows = pl.ds(r, local, stride=group)
            parts.append(jnp.concatenate([source[rows, :] for source in sources], axis=0))
        value = left_product(ahead_ref[...], jnp.concatenate(parts, axis=1))
        value = left_product(back_ref[...], value * jnp.concatenate(kernel, axis=1))
        for d in range(slabs):
            for r in range(8):
                results[d][pl.ds(first + r, local, stride=group), :] = value[
                    d * local : (d + 1) * local, r * LANES : (r + 1) * LANES
                ]


def middle(spectra, wave, along_z, ahead, back, scale, group=40):
    slabs = len(spectra)
    chunks, planes, rows, _ = spectra[0].shape
    block = pl.BlockSpec((chunks, planes, group, LANES), lambda i: (0, 0, i, 0))
    whole = lambda i: (0, 0)

    def kernel(*refs):
        middle_kernel(scale, slabs, *refs)

    return pl.pallas_call(
        kernel,
        grid=(rows // group,),
        in_specs=[block] * slabs
        + [
            pl.BlockSpec((group, LANES), lambda i: (i, 0)),
            pl.BlockSpec(along_z.shape, whole),
            pl.BlockSpec(ahead.shape, whole),
            pl.BlockSpec(back.shape, whole),
        ],
        out_specs=[block] * slabs,
        out_shape=[jax.ShapeDtypeStruct(x.shape, f32) for x in spectra],
        input_output_aliases={d: d for d in range(slabs)},
        cost_estimate=costs(chunks * planes * slabs, rows, 8 * slabs * spectra[0].size),
        compiler_params=pltpu.CompilerParams(vmem_limit_bytes=VMEM),
    )(*spectra, wave, along_z, ahead, back)


def backward_kernel(width, count, *refs):
    v_refs, p_refs, (right_ref, left_ref, o_ref) = refs[:2], refs[2:-3], refs[-3:]
    right, left = right_ref[...], left_ref[...]
    lhs = []
    for n in range(count):
        for j in range(2):
            packed = v_refs[j][n, 0]
            value = jnp.concatenate([packed[:width], spread_tails(packed[width:])], axis=1)
            value = left_product(left, value)
            lhs.append(right_operand(value[:, :LANES], value[:, LANES:]))
    values = jnp.dot(jnp.concatenate(lhs, axis=0), right, preferred_element_type=f32)
    for n in range(count):
        main, tail = 0.0, 0.0
        for j in range(2):
            m = 2 * n + j
            value = values[m * width : (m + 1) * width]
            partner = p_refs[j * count + n][0, 0].astype(f32)
            main = main + value[:, :LANES] * partner[:width]
            tail = tail + gather_tails(value[:, LANES:]) * partner[width:]
        o_ref[n, 0, :width, :] = main.astype(bf16)
        o_ref[n, 0, width:, :] = tail.astype(bf16)


def backward(potentials, partners, right, left, first, steps, width):
    count, planes, rows, _ = potentials[0].shape
    whole = lambda i: (0, 0)

    def of(part):
        return pl.BlockSpec((1, 1, rows, LANES), lambda i: (part, first + i, 0, 0))

    def kernel(*refs):
        backward_kernel(width, count, *refs)

    shape = (count, steps, rows, LANES)
    return pl.pallas_call(
        kernel,
        grid=(steps,),
        in_specs=[pl.BlockSpec((count, 1, rows, LANES), lambda i: (0, first + i, 0, 0))] * 2
        + [of(part) for partner in partners for _, part in partner]
        + [pl.BlockSpec(right.shape, whole), pl.BlockSpec(left.shape, whole)],
        out_specs=pl.BlockSpec((count, 1, rows, LANES), lambda i: (0, i, 0, 0)),
        out_shape=jax.ShapeDtypeStruct(shape, bf16),
        cost_estimate=costs(2 * count * steps, width, 14 * math.prod(shape)),
        compiler_params=pltpu.CompilerParams(vmem_limit_bytes=VMEM),
    )(*potentials, *[array for partner in partners for array, _ in partner], right, left)


def unpack_kernel(parts, pick_ref, *refs):
    x_refs, o_ref = refs[:parts], refs[-1]
    width = o_ref.shape[2]
    planes = [(ref, p) for ref in x_refs for p in range(ref.shape[1])]
    for n, (x_ref, p) in enumerate(planes):
        o_ref[0, n, :, :LANES] = x_ref[0, p, :width, :]
        packed = x_ref[0, p, width:, :].astype(f32)
        turned = [packed] + [pltpu.roll(packed, LANES - TAIL * q, axis=1) for q in range(1, FOLD)]
        tails = jnp.concatenate(turned, axis=0).astype(bf16)
        o_ref[0, n, :, LANES:] = tails[:, :TAIL]


def unpack(pieces, picks, held, shape):
    block, depth, width, across = shape
    count, _, rows, _ = pieces[0].shape
    planes = depth // count
    in_specs = [
        pl.BlockSpec((1, piece.shape[1], rows, LANES), lambda n, w: (n, 0, 0, 0))
        for piece in pieces
    ]
    args, alias = list(pieces), {}
    if held is not None:
        in_specs.append(pl.BlockSpec(memory_space=pl.ANY))
        args.append(held)
        alias = {len(args): 0}

    def kernel(*refs):
        unpack_kernel(len(pieces), *refs)

    return pl.pallas_call(
        kernel,
        grid_spec=pltpu.PrefetchScalarGridSpec(
            num_scalar_prefetch=1,
            grid=(count,),
            in_specs=in_specs,
            out_specs=pl.BlockSpec(
                (1, planes, width, across), lambda n, w: (w[0], w[1 + n], 0, 0)
            ),
        ),
        out_shape=jax.ShapeDtypeStruct(shape, bf16),
        input_output_aliases=alias,
        cost_estimate=pl.CostEstimate(
            flops=0, bytes_accessed=16 * math.prod(pieces[0].shape), transcendentals=0
        ),
        compiler_params=pltpu.CompilerParams(vmem_limit_bytes=VMEM),
    )(picks, *args)


def swap(value, bit):
    count = lax.axis_size("slab")
    return lax.ppermute(value, "slab", [(i, i ^ bit) for i in range(count)])


def ring_order(count):
    return list(range(0, count, 2)) + list(range(count - 1, 0, -2))


def turn(value, step):
    order = ring_order(lax.axis_size("band"))
    count = len(order)
    pairs = [(order[i], order[(i + step) % count]) for i in range(count)]
    return lax.ppermute(value, "band", pairs)


def after(value, *others):
    return lax.optimization_barrier((value, *others))[0]


def scatter(piece, source, place, count, first):
    planes = piece.shape[0] // count

    def own(offset):
        chunk = (place + offset) % count
        return lax.dynamic_slice_in_dim(piece, chunk * planes, planes, 0)

    mine = source == place
    ahead, behind = count // 2, count - count // 2 - 1
    up, down = own(ahead), own(-behind)
    for hop in range(1, ahead + 1):
        up = turn(up, 1)
        if hop == 1:
            up = after(up, first)
        up = jnp.where(mine, own(ahead - hop), up)
        if hop <= behind:
            down = turn(down, -1)
            if hop < behind:
                down = jnp.where(mine, own(hop - behind), down)
    distance = (source - place) % count
    return jnp.where((distance >= 1) & (distance <= behind), down, up)


def scatter_last(piece, place, order):
    count = len(order)
    planes = piece.shape[0] // count
    last = count - 1
    here = order.index(last)
    chunk = piece[here * planes : (here + 1) * planes]
    for n, band in enumerate(order):
        if band != last:
            sent = lax.ppermute(piece[n * planes : (n + 1) * planes], "band", [(last, band)])
            chunk = jnp.where(place == n, sent, chunk)
    return chunk


def whole_orbital(orbitals, owner, index):
    block, depth_local, width, across = orbitals.shape
    slabs, bands = lax.axis_size("slab"), lax.axis_size("band")
    depth = depth_local * slabs
    planes = depth_local // bands
    me, band = lax.axis_index("slab"), lax.axis_index("band")
    order = ring_order(bands)
    ring = jnp.asarray(np.argsort(order).astype(np.int32))
    place = ring[band]
    offsets = [0] + [o for hop in range(1, bands // 2) for o in (-hop, hop)] + [bands // 2]
    places = (place + jnp.asarray(np.array(offsets, np.int32))) % bands

    right = jnp.asarray(right_table(across))
    high, low = split_np(cas_np(width))
    left = jnp.asarray(np.concatenate([high, high, low], axis=1))
    high, low = split_np(cas_np(depth))
    wave = jnp.asarray(packed_wave(width, across))
    along_z = jnp.asarray(np.tile(wave_np(depth)[:, None], (1, LANES)).astype(np.float32))
    turned = me ^ jnp.arange(slabs, dtype=jnp.int32)
    plane = jnp.arange(planes, dtype=jnp.int32)
    z = turned[:, None, None] * depth_local + places[None, :, None] * planes + plane
    z = z.reshape(depth)

    def in_columns(table):
        return jnp.take(jnp.asarray(table), z, axis=1)

    def in_rows(table):
        return jnp.take(jnp.asarray(table), z, axis=0)

    ahead = jnp.concatenate([in_columns(high), in_columns(high), in_columns(low)], axis=1)
    back = jnp.concatenate([in_rows(high), in_rows(high), in_rows(low)], axis=1)

    swapped = owner[0] != bands - 1
    owner = jnp.where(swapped, owner[::-1], owner)
    index = jnp.where(swapped, index[::-1], index)
    candidates = pack(orbitals, index)
    pieces = pack(orbitals, turned)
    half = depth_local // 2
    chunks = [
        scatter_last(candidates[0], place, order),
        scatter(candidates[1], ring[owner[1]], place, bands, pieces[0]),
    ]
    early = swap(pieces[2][:half], 2)
    crossed = [swap(chunks[0], 2)]
    late = swap(after(pieces[2][half:], crossed[0]), 2)
    far = [swap(after(pieces[3][:half], late), 3)]
    crossed.append(swap(chunks[1], 2))
    far.append(swap(after(pieces[3][half:], crossed[1], far[0]), 3))
    orbital = [
        pieces[0],
        swap(pieces[1], 1),
        jnp.concatenate([early, late]),
        jnp.concatenate(far),
    ]

    spectra, partners, potentials = [], [], []
    scale = -0.25 * 4.0 * math.pi / (depth * width * across)
    for j in range(2):
        unit = jnp.stack([chunks[j], crossed[j]])
        up, down = unit, unit
        near = [unit]
        ahead_of = ({2: early, 3: late}, {1: far[0], **dict(zip((2, 3, 4), spectra))})[j]
        for hop in range(1, bands // 2 + 1):
            held = ahead_of.get(hop)
            if held is not None:
                up, down = after(up, held), after(down, held)
            if hop < bands // 2:
                up, down = turn(up, 1), turn(down, -1)
                near += [up, down]
        last = [turn(up[:1], 1), turn(down[1:], -1)]
        other = [swap(value, 1) for value in near]
        other_last = [swap(value, 1) for value in last]
        partner = []
        for d in range(slabs):
            arrays, ends = ((near, last), (other, other_last))[d % 2]
            partner.append([(array, d // 2) for array in arrays] + [(ends[d // 2], 0)])
        partners.append(partner)
        spectra = [forward(places, orbital[d], partner[d], right, left, width) for d in range(slabs)]
        potentials.append(middle(spectra, wave, along_z, ahead, back, scale))

    done = {}
    split = planes // 2
    for d in (2, 3, 1, 0):
        pair = [potentials[j][d] for j in range(2)]
        held = [partners[j][d] for j in range(2)]
        done[d] = []
        for first, steps in ((0, split), (split, planes - split)) if d > 1 else ((0, planes),):
            total = backward(pair, held, right, left, first, steps, width)
            done[d].append(swap(total, d) if d else total)
    out = None
    for d in range(slabs):
        picks = jnp.concatenate([turned[d : d + 1], places])
        out = unpack(done[d], picks, out, orbitals.shape)
    return out


def spread(block, axis, source):
    block = jnp.where(lax.axis_index(axis) == source, block, jnp.zeros_like(block))
    return lax.psum(block, axis)


def cas_table(count):
    steps = jnp.arange(count, dtype=jnp.int32)
    product = steps[:, None] * steps[None, :] % count
    angle = 2.0 * math.pi / count * product.astype(jnp.float32)
    return jnp.cos(angle) + jnp.sin(angle)


def squared_wave(steps, count):
    folded = jnp.where(steps <= count // 2, steps, steps - count).astype(jnp.float32)
    wave = 2.0 * math.pi * folded / (count * spacing)
    return wave * wave


def coulomb_slice(depth, first, width, across):
    along_z = squared_wave(jnp.arange(depth, dtype=jnp.int32), depth)
    along_x = squared_wave(
        first + jnp.arange(width, dtype=jnp.int32), width * lax.axis_size("slab")
    )
    along_y = squared_wave(jnp.arange(across, dtype=jnp.int32), across)
    g_sq = along_z[:, None, None] + along_x[None, :, None] + along_y[None, None, :]
    safe = jnp.where(g_sq > 0, g_sq, jnp.float32(1.0))
    whole = depth * width * lax.axis_size("slab") * across
    return jnp.where(g_sq > 0, 4.0 * math.pi / safe, jnp.float32(0.0)) / whole


def along_x(grid, table):
    return jnp.einsum(
        "pzxy,xk->pzky", grid, table, precision=exact, preferred_element_type=jnp.float32
    )


def along_y(grid, table):
    return jnp.einsum(
        "pzxy,yk->pzxk", grid, table, precision=exact, preferred_element_type=jnp.float32
    )


def along_z(grid, table):
    return jnp.einsum(
        "pzxy,zk->pkxy", grid, table, precision=exact, preferred_element_type=jnp.float32
    )


def fetch(orbitals, owner, index, which):
    local = lax.dynamic_index_in_dim(orbitals, index[which], 0, keepdims=False)
    return spread(local, "band", owner[which])


def solve(density, tables, kernel):
    table_x, table_y, table_z = tables
    spectrum = along_x(density, table_x)
    spectrum = along_y(spectrum, table_y)
    scaled = (
        along_z(lax.all_to_all(spectrum, "slab", split_axis=2, concat_axis=1, tiled=True), table_z)
        * kernel[None]
    )
    back = along_z(scaled, table_z)
    potential = lax.all_to_all(back, "slab", split_axis=1, concat_axis=2, tiled=True)
    potential = along_y(potential, table_y)
    return along_x(potential, table_x)


def split_orbital(orbitals, owner, index):
    block, depth_local, width, across = orbitals.shape
    slabs = lax.axis_size("slab")
    depth = depth_local * slabs
    width_local = width // slabs
    tables = (cas_table(width), cas_table(across), cas_table(depth))
    first = lax.axis_index("slab") * width_local
    kernel = coulomb_slice(depth, first, width_local, across)
    bands = orbitals.astype(jnp.float32)
    total = jnp.zeros(orbitals.shape, jnp.float32)
    for which in range(2):
        partner = fetch(orbitals, owner, index, which).astype(jnp.float32)
        potential = solve(bands * partner[None], tables, kernel)
        total = total + partner[None] * potential
    return (-0.25 * total).astype(jnp.bfloat16)


def per_device(orbitals, owner, index):
    block, depth_local, width, across = orbitals.shape
    slabs, bands = lax.axis_size("slab"), lax.axis_size("band")
    fits = (
        block == slabs == 4
        and bands % 2 == 0
        and depth_local % bands == 0
        and depth_local % 8 == 0
        and across == LANES + TAIL
        and width % (8 * FOLD) == 0
    )
    return (whole_orbital if fits else split_orbital)(orbitals, owner, index)


def solution(mesh):
    placed = (P("band", "slab", None, None), P(), P())
    return jax.shard_map(
        per_device,
        mesh=mesh,
        in_specs=placed,
        out_specs=P("band", "slab", None, None),
        check_vma=False,
    )
```

```python
import math

import jax
import jax.numpy as jnp
import ml_dtypes
import numpy as np
from jax import lax
from jax.experimental import pallas as pl
from jax.experimental.pallas import tpu as pltpu
from jax.sharding import PartitionSpec as P

spacing = 0.293125
exact = lax.Precision.HIGHEST
LANES = 128
TAIL = 32
FOLD = LANES // TAIL
VMEM = 56 * 2**20
bf16, f32 = jnp.bfloat16, jnp.float32


def cas_np(count):
    steps = np.arange(count)
    angle = 2.0 * np.pi / count * (steps[:, None] * steps[None, :] % count)
    return np.cos(angle) + np.sin(angle)


def split_np(table):
    high = table.astype(ml_dtypes.bfloat16)
    low = (table - high.astype(np.float64)).astype(ml_dtypes.bfloat16)
    return high, low


def wave_np(count):
    steps = np.arange(count)
    folded = np.where(steps <= count // 2, steps, steps - count)
    return (2.0 * np.pi * folded / (count * spacing)) ** 2


def right_table(count):
    high, low = split_np(cas_np(count))
    wide = [np.concatenate([t[:, :LANES]] + [t[:, LANES:]] * FOLD, axis=1) for t in (high, low)]
    high, low = wide
    zero = np.zeros_like(high[LANES:])
    return np.concatenate(
        [high[:LANES], high[:LANES], low[:LANES], high[LANES:], high[LANES:], low[LANES:], zero]
    )


def packed_wave(width, across):
    sq = wave_np(width)[:, None] + wave_np(across)[None, :]
    tails = sq[:, LANES:].reshape(FOLD, width // FOLD, TAIL).transpose(1, 0, 2)
    return np.concatenate([sq[:, :LANES], tails.reshape(width // FOLD, LANES)]).astype(np.float32)


def halves(value):
    high = value.astype(bf16)
    low = (value - high.astype(f32)).astype(bf16)
    return high, low


def lane_group():
    return lax.broadcasted_iota(jnp.int32, (1, LANES), 1) // TAIL


def spread_tails(packed):
    group = lane_group()
    turned = [packed] + [pltpu.roll(packed, TAIL * k, axis=1) for k in range(1, FOLD)]
    out = []
    for q in range(FOLD):
        rows = turned[(0 - q) % FOLD]
        for g in range(1, FOLD):
            rows = jnp.where(group == g, turned[(g - q) % FOLD], rows)
        out.append(rows)
    return jnp.concatenate(out, axis=0)


def gather_tails(tails):
    group = lane_group()
    rows = tails.shape[0] // FOLD
    packed = tails[:rows]
    for q in range(1, FOLD):
        packed = jnp.where(group == q, tails[q * rows : (q + 1) * rows], packed)
    return packed


def right_operand(main, tails):
    high, low = halves(main)
    coarse = tails.astype(bf16).astype(f32)
    mixed = (tails - jnp.where(lane_group() == 1, coarse, 0.0)).astype(bf16)
    return jnp.concatenate([high, low, high, mixed], axis=1)


def left_product(table, value):
    high, low = halves(value)
    stacked = jnp.concatenate([high, low, high], axis=0)
    return jnp.dot(table, stacked, preferred_element_type=f32)


def pack_kernel(pick_ref, *refs):
    count = len(refs) // 2
    planes, width = refs[0].shape[1], refs[0].shape[2]
    lane = lax.broadcasted_iota(jnp.int32, (TAIL, LANES), 1)
    row = lax.broadcasted_iota(jnp.int32, (TAIL, LANES), 0)
    place = (lane % TAIL == row).astype(f32).astype(bf16)
    for x_ref, o_ref in zip(refs[:count], refs[count:]):
        tails = x_ref[0, :, :, LANES:].reshape(planes * width, TAIL)
        tails = jnp.dot(tails, place, preferred_element_type=f32)
        for p in range(planes):
            o_ref[p, :width, :] = x_ref[0, p, :, :LANES]
            o_ref[p, width:, :] = gather_tails(tails[p * width : (p + 1) * width]).astype(bf16)


def pack(orbitals, picks, planes=20):
    block, depth, width, across = orbitals.shape
    rows = width + width // FOLD
    count = picks.shape[0]

    def picked(n):
        return pl.BlockSpec((1, planes, width, across), lambda i, p: (p[n], i, 0, 0))

    return pl.pallas_call(
        pack_kernel,
        grid_spec=pltpu.PrefetchScalarGridSpec(
            num_scalar_prefetch=1,
            grid=(depth // planes,),
            in_specs=[picked(n) for n in range(count)],
            out_specs=[pl.BlockSpec((planes, rows, LANES), lambda i, p: (i, 0, 0))] * count,
        ),
        out_shape=[jax.ShapeDtypeStruct((depth, rows, LANES), bf16)] * count,
        compiler_params=pltpu.CompilerParams(vmem_limit_bytes=VMEM),
    )(picks, *[orbitals] * count)


def forward_kernel(width, count, places_ref, *refs):
    o_refs, p_refs, (right_ref, left_ref, s_ref) = refs[:count], refs[count : 2 * count], refs[-3:]
    right, left = right_ref[...], left_ref[...]
    lhs = []
    for o_ref, p_ref in zip(o_refs, p_refs):
        density = o_ref[0].astype(f32) * p_ref[0, 0].astype(f32)
        lhs.append(right_operand(density[:width], spread_tails(density[width:])))
    for n in range(count):
        along_y = jnp.dot(lhs[n], right, preferred_element_type=f32)
        value = left_product(left, along_y)
        s_ref[n, 0, :width, :] = value[:, :LANES]
        s_ref[n, 0, width:, :] = gather_tails(value[:, LANES:])


def costs(pairs, width, moved):
    flops = int(pairs * width * 2 * 2 * 3 * 256 * 160 * 1.5)
    return pl.CostEstimate(flops=flops, bytes_accessed=int(moved), transcendentals=0)


def forward(places, orbital, partner, right, left, width):
    rows = orbital.shape[1]
    count, planes = len(partner), partner[0][0].shape[1]
    whole = lambda i, c: (0, 0)

    def at(n):
        return pl.BlockSpec((1, rows, LANES), lambda i, c: (c[n] * planes + i, 0, 0))

    def of(part):
        return pl.BlockSpec((1, 1, rows, LANES), lambda i, c: (part, i, 0, 0))

    def kernel(*refs):
        forward_kernel(width, count, *refs)

    shape = (count, planes, rows, LANES)
    return pl.pallas_call(
        kernel,
        grid_spec=pltpu.PrefetchScalarGridSpec(
            num_scalar_prefetch=1,
            grid=(planes,),
            in_specs=[at(n) for n in range(count)]
            + [of(part) for _, part in partner]
            + [pl.BlockSpec(right.shape, whole), pl.BlockSpec(left.shape, whole)],
            out_specs=pl.BlockSpec((count, 1, rows, LANES), lambda i, c: (0, i, 0, 0)),
        ),
        out_shape=jax.ShapeDtypeStruct(shape, f32),
        cost_estimate=costs(count * planes, width, 8 * math.prod(shape)),
        compiler_params=pltpu.CompilerParams(vmem_limit_bytes=VMEM),
    )(places, *[orbital] * count, *[array for array, _ in partner], right, left)


def middle_kernel(scale, slabs, *refs):
    x_refs, (wave_ref, depth_ref, ahead_ref, back_ref) = refs[:slabs], refs[slabs : slabs + 4]
    o_refs = refs[slabs + 4 :]
    chunks, planes, group, _ = x_refs[0].shape
    local = chunks * planes
    along_z = depth_ref[...]
    sources = [ref.reshape(local * group, LANES) for ref in x_refs]
    results = [ref.reshape(local * group, LANES) for ref in o_refs]
    for first in range(0, group, 8):
        kernel, parts = [], []
        for r in range(first, first + 8):
            g_sq = along_z + wave_ref[r : r + 1, :]
            safe = jnp.where(g_sq > 0, g_sq, 1.0)
            kernel.append(jnp.where(g_sq > 0, scale / safe, 0.0))
            rows = pl.ds(r, local, stride=group)
            parts.append(jnp.concatenate([source[rows, :] for source in sources], axis=0))
        value = left_product(ahead_ref[...], jnp.concatenate(parts, axis=1))
        value = left_product(back_ref[...], value * jnp.concatenate(kernel, axis=1))
        for d in range(slabs):
            for r in range(8):
                results[d][pl.ds(first + r, local, stride=group), :] = value[
                    d * local : (d + 1) * local, r * LANES : (r + 1) * LANES
                ]


def middle(spectra, wave, along_z, ahead, back, scale, group=40):
    slabs = len(spectra)
    chunks, planes, rows, _ = spectra[0].shape
    block = pl.BlockSpec((chunks, planes, group, LANES), lambda i: (0, 0, i, 0))
    whole = lambda i: (0, 0)

    def kernel(*refs):
        middle_kernel(scale, slabs, *refs)

    return pl.pallas_call(
        kernel,
        grid=(rows // group,),
        in_specs=[block] * slabs
        + [
            pl.BlockSpec((group, LANES), lambda i: (i, 0)),
            pl.BlockSpec(along_z.shape, whole),
            pl.BlockSpec(ahead.shape, whole),
            pl.BlockSpec(back.shape, whole),
        ],
        out_specs=[block] * slabs,
        out_shape=[jax.ShapeDtypeStruct(x.shape, f32) for x in spectra],
        input_output_aliases={d: d for d in range(slabs)},
        cost_estimate=costs(chunks * planes * slabs, rows, 8 * slabs * spectra[0].size),
        compiler_params=pltpu.CompilerParams(vmem_limit_bytes=VMEM),
    )(*spectra, wave, along_z, ahead, back)


def backward_kernel(width, count, *refs):
    v_refs, p_refs, (right_ref, left_ref, o_ref) = refs[:2], refs[2:-3], refs[-3:]
    right, left = right_ref[...], left_ref[...]
    lhs = []
    for n in range(count):
        for j in range(2):
            packed = v_refs[j][n, 0]
            value = jnp.concatenate([packed[:width], spread_tails(packed[width:])], axis=1)
            value = left_product(left, value)
            lhs.append(right_operand(value[:, :LANES], value[:, LANES:]))
    values = jnp.dot(jnp.concatenate(lhs, axis=0), right, preferred_element_type=f32)
    for n in range(count):
        main, tail = 0.0, 0.0
        for j in range(2):
            m = 2 * n + j
            value = values[m * width : (m + 1) * width]
            partner = p_refs[j * count + n][0, 0].astype(f32)
            main = main + value[:, :LANES] * partner[:width]
            tail = tail + gather_tails(value[:, LANES:]) * partner[width:]
        o_ref[n, 0, :width, :] = main.astype(bf16)
        o_ref[n, 0, width:, :] = tail.astype(bf16)


def backward(potentials, partners, right, left, first, steps, width):
    count, planes, rows, _ = potentials[0].shape
    whole = lambda i: (0, 0)

    def of(part):
        return pl.BlockSpec((1, 1, rows, LANES), lambda i: (part, first + i, 0, 0))

    def kernel(*refs):
        backward_kernel(width, count, *refs)

    shape = (count, steps, rows, LANES)
    return pl.pallas_call(
        kernel,
        grid=(steps,),
        in_specs=[pl.BlockSpec((count, 1, rows, LANES), lambda i: (0, first + i, 0, 0))] * 2
        + [of(part) for partner in partners for _, part in partner]
        + [pl.BlockSpec(right.shape, whole), pl.BlockSpec(left.shape, whole)],
        out_specs=pl.BlockSpec((count, 1, rows, LANES), lambda i: (0, i, 0, 0)),
        out_shape=jax.ShapeDtypeStruct(shape, bf16),
        cost_estimate=costs(2 * count * steps, width, 14 * math.prod(shape)),
        compiler_params=pltpu.CompilerParams(vmem_limit_bytes=VMEM),
    )(*potentials, *[array for partner in partners for array, _ in partner], right, left)


def unpack_kernel(parts, pick_ref, *refs):
    x_refs, o_ref = refs[:parts], refs[-1]
    width = o_ref.shape[2]
    planes = [(ref, p) for ref in x_refs for p in range(ref.shape[1])]
    for n, (x_ref, p) in enumerate(planes):
        o_ref[0, n, :, :LANES] = x_ref[0, p, :width, :]
        packed = x_ref[0, p, width:, :].astype(f32)
        turned = [packed] + [pltpu.roll(packed, LANES - TAIL * q, axis=1) for q in range(1, FOLD)]
        tails = jnp.concatenate(turned, axis=0).astype(bf16)
        o_ref[0, n, :, LANES:] = tails[:, :TAIL]


def unpack(pieces, picks, held, shape):
    block, depth, width, across = shape
    count, _, rows, _ = pieces[0].shape
    planes = depth // count
    in_specs = [
        pl.BlockSpec((1, piece.shape[1], rows, LANES), lambda n, w: (n, 0, 0, 0))
        for piece in pieces
    ]
    args, alias = list(pieces), {}
    if held is not None:
        in_specs.append(pl.BlockSpec(memory_space=pl.ANY))
        args.append(held)
        alias = {len(args): 0}

    def kernel(*refs):
        unpack_kernel(len(pieces), *refs)

    return pl.pallas_call(
        kernel,
        grid_spec=pltpu.PrefetchScalarGridSpec(
            num_scalar_prefetch=1,
            grid=(count,),
            in_specs=in_specs,
            out_specs=pl.BlockSpec(
                (1, planes, width, across), lambda n, w: (w[0], w[1 + n], 0, 0)
            ),
        ),
        out_shape=jax.ShapeDtypeStruct(shape, bf16),
        input_output_aliases=alias,
        cost_estimate=pl.CostEstimate(
            flops=0, bytes_accessed=16 * math.prod(pieces[0].shape), transcendentals=0
        ),
        compiler_params=pltpu.CompilerParams(vmem_limit_bytes=VMEM),
    )(picks, *args)


def swap(value, bit):
    count = lax.axis_size("slab")
    return lax.ppermute(value, "slab", [(i, i ^ bit) for i in range(count)])


def ring_order(count):
    return list(range(0, count, 2)) + list(range(count - 1, 0, -2))


def turn(value, step):
    order = ring_order(lax.axis_size("band"))
    count = len(order)
    pairs = [(order[i], order[(i + step) % count]) for i in range(count)]
    return lax.ppermute(value, "band", pairs)


def after(value, *others):
    return lax.optimization_barrier((value, *others))[0]


def scatter(piece, source, place, count, first):
    planes = piece.shape[0] // count

    def own(offset):
        chunk = (place + offset) % count
        return lax.dynamic_slice_in_dim(piece, chunk * planes, planes, 0)

    mine = source == place
    ahead, behind = count // 2, count - count // 2 - 1
    up, down = own(ahead), own(-behind)
    for hop in range(1, ahead + 1):
        up = turn(up, 1)
        if hop == 1:
            up = after(up, first)
        up = jnp.where(mine, own(ahead - hop), up)
        if hop <= behind:
            down = turn(down, -1)
            if hop < behind:
                down = jnp.where(mine, own(hop - behind), down)
    distance = (source - place) % count
    return jnp.where((distance >= 1) & (distance <= behind), down, up)


def scatter_last(piece, place, order):
    count = len(order)
    planes = piece.shape[0] // count
    last = count - 1
    here = order.index(last)
    chunk = piece[here * planes : (here + 1) * planes]
    for n, band in enumerate(order):
        if band != last:
            sent = lax.ppermute(piece[n * planes : (n + 1) * planes], "band", [(last, band)])
            chunk = jnp.where(place == n, sent, chunk)
    return chunk


def whole_orbital(orbitals, owner, index):
    block, depth_local, width, across = orbitals.shape
    slabs, bands = lax.axis_size("slab"), lax.axis_size("band")
    depth = depth_local * slabs
    planes = depth_local // bands
    me, band = lax.axis_index("slab"), lax.axis_index("band")
    order = ring_order(bands)
    ring = jnp.asarray(np.argsort(order).astype(np.int32))
    place = ring[band]
    offsets = [0] + [o for hop in range(1, bands // 2) for o in (-hop, hop)] + [bands // 2]
    places = (place + jnp.asarray(np.array(offsets, np.int32))) % bands

    right = jnp.asarray(right_table(across))
    high, low = split_np(cas_np(width))
    left = jnp.asarray(np.concatenate([high, high, low], axis=1))
    high, low = split_np(cas_np(depth))
    wave = jnp.asarray(packed_wave(width, across))
    along_z = jnp.asarray(np.tile(wave_np(depth)[:, None], (1, LANES)).astype(np.float32))
    turned = me ^ jnp.arange(slabs, dtype=jnp.int32)
    plane = jnp.arange(planes, dtype=jnp.int32)
    z = turned[:, None, None] * depth_local + places[None, :, None] * planes + plane
    z = z.reshape(depth)

    def in_columns(table):
        return jnp.take(jnp.asarray(table), z, axis=1)

    def in_rows(table):
        return jnp.take(jnp.asarray(table), z, axis=0)

    ahead = jnp.concatenate([in_columns(high), in_columns(high), in_columns(low)], axis=1)
    back = jnp.concatenate([in_rows(high), in_rows(high), in_rows(low)], axis=1)

    swapped = owner[0] != bands - 1
    owner = jnp.where(swapped, owner[::-1], owner)
    index = jnp.where(swapped, index[::-1], index)
    candidates = pack(orbitals, index)
    pieces = pack(orbitals, turned)
    half = depth_local // 2
    chunks = [
        scatter_last(candidates[0], place, order),
        scatter(candidates[1], ring[owner[1]], place, bands, pieces[0]),
    ]
    early = swap(pieces[2][:half], 2)
    crossed = [swap(chunks[0], 2)]
    late = swap(after(pieces[2][half:], crossed[0]), 2)
    far = [swap(after(pieces[3][:half], late), 3)]
    crossed.append(swap(chunks[1], 2))
    far.append(swap(after(pieces[3][half:], crossed[1], far[0]), 3))
    orbital = [
        pieces[0],
        swap(pieces[1], 1),
        jnp.concatenate([early, late]),
        jnp.concatenate(far),
    ]

    spectra, partners, potentials = [], [], []
    scale = -0.25 * 4.0 * math.pi / (depth * width * across)
    for j in range(2):
        unit = jnp.stack([chunks[j], crossed[j]])
        up, down = unit, unit
        near = [unit]
        ahead_of = ({2: early, 3: late}, {1: far[0], **dict(zip((2, 3, 4), spectra))})[j]
        for hop in range(1, bands // 2 + 1):
            held = ahead_of.get(hop)
            if held is not None:
                up, down = after(up, held), after(down, held)
            if hop < bands // 2:
                up, down = turn(up, 1), turn(down, -1)
                near += [up, down]
        last = [turn(up[:1], 1), turn(down[1:], -1)]
        other = [swap(value, 1) for value in near]
        other_last = [swap(value, 1) for value in last]
        partner = []
        for d in range(slabs):
            arrays, ends = ((near, last), (other, other_last))[d % 2]
            partner.append([(array, d // 2) for array in arrays] + [(ends[d // 2], 0)])
        partners.append(partner)
        spectra = [forward(places, orbital[d], partner[d], right, left, width) for d in range(slabs)]
        potentials.append(middle(spectra, wave, along_z, ahead, back, scale))

    done = {}
    split = planes // 2
    for d in (2, 3, 0, 1):
        pair = [potentials[j][d] for j in range(2)]
        held = [partners[j][d] for j in range(2)]
        done[d] = []
        if d == 1:
            pair[0] = after(pair[0], done[0][0])
        for first, steps in ((0, split), (split, planes - split)) if d > 1 else ((0, planes),):
            total = backward(pair, held, right, left, first, steps, width)
            done[d].append(swap(total, d) if d else total)
    out = None
    for d in range(slabs):
        picks = jnp.concatenate([turned[d : d + 1], places])
        out = unpack(done[d], picks, out, orbitals.shape)
    return out


def spread(block, axis, source):
    block = jnp.where(lax.axis_index(axis) == source, block, jnp.zeros_like(block))
    return lax.psum(block, axis)


def cas_table(count):
    steps = jnp.arange(count, dtype=jnp.int32)
    product = steps[:, None] * steps[None, :] % count
    angle = 2.0 * math.pi / count * product.astype(jnp.float32)
    return jnp.cos(angle) + jnp.sin(angle)


def squared_wave(steps, count):
    folded = jnp.where(steps <= count // 2, steps, steps - count).astype(jnp.float32)
    wave = 2.0 * math.pi * folded / (count * spacing)
    return wave * wave


def coulomb_slice(depth, first, width, across):
    along_z = squared_wave(jnp.arange(depth, dtype=jnp.int32), depth)
    along_x = squared_wave(
        first + jnp.arange(width, dtype=jnp.int32), width * lax.axis_size("slab")
    )
    along_y = squared_wave(jnp.arange(across, dtype=jnp.int32), across)
    g_sq = along_z[:, None, None] + along_x[None, :, None] + along_y[None, None, :]
    safe = jnp.where(g_sq > 0, g_sq, jnp.float32(1.0))
    whole = depth * width * lax.axis_size("slab") * across
    return jnp.where(g_sq > 0, 4.0 * math.pi / safe, jnp.float32(0.0)) / whole


def along_x(grid, table):
    return jnp.einsum(
        "pzxy,xk->pzky", grid, table, precision=exact, preferred_element_type=jnp.float32
    )


def along_y(grid, table):
    return jnp.einsum(
        "pzxy,yk->pzxk", grid, table, precision=exact, preferred_element_type=jnp.float32
    )


def along_z(grid, table):
    return jnp.einsum(
        "pzxy,zk->pkxy", grid, table, precision=exact, preferred_element_type=jnp.float32
    )


def fetch(orbitals, owner, index, which):
    local = lax.dynamic_index_in_dim(orbitals, index[which], 0, keepdims=False)
    return spread(local, "band", owner[which])


def solve(density, tables, kernel):
    table_x, table_y, table_z = tables
    spectrum = along_x(density, table_x)
    spectrum = along_y(spectrum, table_y)
    scaled = (
        along_z(lax.all_to_all(spectrum, "slab", split_axis=2, concat_axis=1, tiled=True), table_z)
        * kernel[None]
    )
    back = along_z(scaled, table_z)
    potential = lax.all_to_all(back, "slab", split_axis=1, concat_axis=2, tiled=True)
    potential = along_y(potential, table_y)
    return along_x(potential, table_x)


def split_orbital(orbitals, owner, index):
    block, depth_local, width, across = orbitals.shape
    slabs = lax.axis_size("slab")
    depth = depth_local * slabs
    width_local = width // slabs
    tables = (cas_table(width), cas_table(across), cas_table(depth))
    first = lax.axis_index("slab") * width_local
    kernel = coulomb_slice(depth, first, width_local, across)
    bands = orbitals.astype(jnp.float32)
    total = jnp.zeros(orbitals.shape, jnp.float32)
    for which in range(2):
        partner = fetch(orbitals, owner, index, which).astype(jnp.float32)
        potential = solve(bands * partner[None], tables, kernel)
        total = total + partner[None] * potential
    return (-0.25 * total).astype(jnp.bfloat16)


def per_device(orbitals, owner, index):
    block, depth_local, width, across = orbitals.shape
    slabs, bands = lax.axis_size("slab"), lax.axis_size("band")
    fits = (
        block == slabs == 4
        and bands % 2 == 0
        and depth_local % bands == 0
        and depth_local % 8 == 0
        and across == LANES + TAIL
        and width % (8 * FOLD) == 0
    )
    return (whole_orbital if fits else split_orbital)(orbitals, owner, index)


def solution(mesh):
    placed = (P("band", "slab", None, None), P(), P())
    return jax.shard_map(
        per_device,
        mesh=mesh,
        in_specs=placed,
        out_specs=P("band", "slab", None, None),
        check_vma=False,
    )
```
